512 devices in a mesh: row: 4 (over y_lo, core), col: 16 (over z), depth: 8 (over x, y_hi).
Axes of the slice: x: 4, y: 4 (y_hi: 2, y_lo: 2; y = y_hi * 2 + y_lo), z: 16, core: 2. Of those that a mesh axis runs over, the one named last changes fastest.
Arguments:
- lower_block: bfloat16 [24576, 2048], P(('col', 'row')), may hold values from -0.3984375 to 0.3984375
- solve_factor: bfloat16 [2048, 2048], P(None, 'depth'), may hold values from -0.125 to 0.125
- schur_window: float32 [2560, 24576], P(('row', 'depth'), 'col'), may hold values from -6 to 6
Outputs:
- schur: float32 [2560, 24576], P(('row', 'depth'), 'col')
The draws below stay inside these ranges and needn't reach their ends.
All inputs are finite; a program needn't handle non-finite values.
Results may differ from the reference program's by a relative error of at most 0.0003.
Values may be sent and summed in bfloat16 or wider, within the bound.
No kernel may reach another device: no remote copies, remote signals or barrier semaphores. Data moves between devices by JAX's collectives and lax.ppermute only.
A program may use at most 64 MiB of HBM per device.

```python
import jax
import jax.numpy as jnp

N = 24576
K = 2048
WIN = 40
GRID_R = 4
GRID_C = 16
SLICES = 8
BLOCK = 384
KS = 256
WINDOW = 2560


def steps_of(rng, shape, cuts, low, high):
    level = 1.0
    for dim, parts in cuts:
        steps = jax.random.uniform(jax.random.fold_in(jax.random.fold_in(rng, 6), dim), (parts,), jnp.float32, low / len(cuts), high / len(cuts))
        level = level * jnp.repeat(jnp.exp(steps), shape[dim] // parts).reshape((-1,) + (1,) * (len(shape) - 1 - dim))
    return level


def gaussian(stream_key, shape, spread, bound, split=(), kind=jnp.bfloat16):
    loudness = steps_of(stream_key, shape, split, -0.22, 0.18) if split else 1.0
    drawn = jax.random.normal(stream_key, shape, jnp.float32) * spread * loudness
    return jnp.minimum(jnp.maximum(drawn, -bound), bound).astype(kind)


def setup_inputs(seed: int = 0) -> dict:
    keys = jax.random.split(jax.random.key(seed), 4)
    lower_block = gaussian(keys[0], (N, K), 0.0571, 0.3984375, ((0, 64),))
    solve_factor = gaussian(keys[1], (K, K), K ** -0.5, 0.125, ((1, 8),))
    schur_window = gaussian(keys[2], (WINDOW, N), 1.0, 6.0, ((0, 32), (1, 16)), jnp.float32)
    return dict(lower_block=lower_block, solve_factor=solve_factor, schur_window=schur_window)


def reference(lower_block, solve_factor, schur_window):
    panel = jnp.dot(lower_block, solve_factor, preferred_element_type=jnp.float32).astype(jnp.bfloat16)
    grouped = panel.reshape(GRID_C, GRID_R, BLOCK, K)[:, :, :WIN, :]
    window_panel = jnp.transpose(grouped, (1, 0, 2, 3)).reshape(WINDOW, K)
    update = jnp.zeros((WINDOW, N), jnp.float32)
    for layer_index in range(SLICES):
        left = window_panel[:, layer_index * KS:(layer_index + 1) * KS]
        right = panel[:, layer_index * KS:(layer_index + 1) * KS]
        product = jnp.dot(left, right.T, preferred_element_type=jnp.float32)
        update = update + product
    return schur_window - update
```

```python
import jax
import jax.numpy as jnp
from jax import lax
from jax.sharding import Mesh, PartitionSpec as P

AXES = ("ylo", "core", "zh", "zl", "x", "yhi")


def spread(block, axes, parts):
    copies = jnp.broadcast_to(block[None], (parts,) + block.shape)
    return lax.all_to_all(copies, axes, 0, 0, tiled=True)


SWAP = ((0, 1), (1, 0))


def shifts(size):
    return [[(i, (i + k) % size) for i in range(size)] for k in range(1, size)]


def on_device(lower_block, solve_factor, schur_window):
    panel = jnp.dot(lower_block, solve_factor, preferred_element_type=jnp.float32).astype(jnp.bfloat16)
    win = 40
    near = spread(panel, ("ylo", "x", "yhi"), 16)
    w = lax.all_gather(panel[:win], "zh")
    w = lax.all_gather(w, "zl")
    w = w.reshape(2, 2, 4, win, 256).transpose(0, 2, 1, 3, 4).reshape(2, 4, 2 * win, 256)
    h = lax.axis_index("yhi")
    got = lax.ppermute(lax.dynamic_index_in_dim(w, 1 - h, 0, False), "yhi", SWAP)
    own = lax.dynamic_index_in_dim(w, h, 0, False)
    lo, hi = jnp.where(h == 0, own, got), jnp.where(h == 0, got, own)
    w = jnp.stack([lo, hi], 1)
    x = lax.axis_index("x")
    parts = [lax.dynamic_index_in_dim(w, x, 0, False)]
    for k, perm in enumerate(shifts(4), 1):
        parts.append(lax.ppermute(lax.dynamic_index_in_dim(w, (x + k) % 4, 0, False), "x", perm))
    w = jnp.stack(parts)
    w = jnp.roll(w[::-1], x + 1, 0).reshape(8, 2 * win, 256)
    other_w = lax.ppermute(w, "core", SWAP)
    near = near.reshape(2, 8, 384, 256)
    rows = jnp.concatenate([w, other_w], 1)
    prod = lax.dot_general(rows, near, (((0, 2), (1, 3)), ((), ())), preferred_element_type=jnp.float32)
    mine = prod[:80]
    theirs = lax.ppermute(prod[80:], "core", SWAP)
    first = lax.axis_index("core") == 0
    update = jnp.stack([jnp.where(first, mine, theirs), jnp.where(first, theirs, mine)], 2)
    return schur_window - update.reshape(schur_window.shape)


def solution(mesh):
    fine = Mesh(mesh.devices.reshape(2, 2, 4, 4, 4, 2), AXES)
    z, row, depth = ("zh", "zl"), ("ylo", "core"), ("x", "yhi")
    out = P(row + depth, z)
    return jax.shard_map(
        on_device, mesh=fine, in_specs=(P(z + row, None), P(None, depth), out), out_specs=out, check_vma=False
    )
```

```python
import jax
import jax.numpy as jnp
from jax import lax
from jax.experimental import pallas as pl
from jax.experimental.pallas import tpu as pltpu
from jax.sharding import Mesh, PartitionSpec as P

AXES = ("ylo", "core", "zh", "zl", "x", "yhi")
WIN = 40
SWAP = ((0, 1), (1, 0))


def product_kernel(at_ref, w, mine, theirs, out_ref, rows_ref):
    h, b = at_ref[0], at_ref[1]
    for p in range(4):
        start = pl.multiple_of(((p // 2 + h) % 2) * 2 * WIN + (p % 2) * WIN, 8)
        for x in range(4):
            rows_ref[x, pl.ds(start, WIN), :] = w[p, x].astype(jnp.float32)
    for a in range(2):
        for t, near in enumerate((mine, theirs)):
            total = None
            for x in range(4):
                term = lax.dot_general(
                    rows_ref[x].astype(jnp.bfloat16), near[a, x], (((1,), (1,)), ((), ())), preferred_element_type=jnp.float32
                )
                total = term if total is None else total + term
            cols = pl.multiple_of(a * 768 + ((b + t) % 2) * 384, 128)
            out_ref[0, :, pl.ds(cols, 384)] = total[:80]
            out_ref[1, :, pl.ds(cols, 384)] = total[80:]


def product(at, w, mine, theirs):
    return pl.pallas_call(
        product_kernel,
        out_shape=jax.ShapeDtypeStruct((2, 2 * WIN, 1536), jnp.float32),
        in_specs=[pl.BlockSpec(memory_space=pltpu.SMEM)] + [pl.BlockSpec(memory_space=pltpu.VMEM)] * 3,
        out_specs=pl.BlockSpec(memory_space=pltpu.VMEM),
        scratch_shapes=[pltpu.VMEM((4, 4 * WIN, 256), jnp.float32)],
        compiler_params=pltpu.CompilerParams(vmem_limit_bytes=32 * 2**20),
        cost_estimate=pl.CostEstimate(flops=2 * 160 * 1536 * 1024, bytes_accessed=4 * 2**20, transcendentals=0),
    )(at, w, mine, theirs)


def spread(block, axes, parts):
    copies = jnp.broadcast_to(block[None], (parts,) + block.shape)
    return lax.all_to_all(copies, axes, 0, 0, tiled=True)


def dot(left, right):
    return jnp.dot(left, right, preferred_element_type=jnp.float32).astype(jnp.bfloat16)


def shift(size, k):
    return [(i, (i + k) % size) for i in range(size)]


def on_device(lower_block, solve_factor, schur_window):
    h, b = lax.axis_index("yhi"), lax.axis_index("core")
    panel = dot(lower_block, solve_factor)
    near = spread(panel, ("ylo", "x"), 8).reshape(2, 4, 384, 256)
    w = lax.all_gather(panel[:WIN], ("zh", "zl"))
    near, w = lax.optimization_barrier((near, w))
    w = w.reshape(4, 4, WIN, 256).transpose(1, 0, 2, 3)
    w = lax.all_to_all(w, "x", 1, 1, tiled=True)
    other = lax.ppermute(near, "core", SWAP)
    out = product(jnp.stack([h, b]), w, near, other)
    return schur_window - (out[0] + lax.ppermute(out[1], "yhi", SWAP))


def solution(mesh):
    fine = Mesh(mesh.devices.reshape(2, 2, 4, 4, 4, 2), AXES)
    z, row, depth = ("zh", "zl"), ("ylo", "core"), ("x", "yhi")
    out = P(row + depth, z)
    return jax.shard_map(
        on_device, mesh=fine, in_specs=(P(z + row, None), P(None, depth), out), out_specs=out, check_vma=False
    )
```

```python
import jax
import jax.numpy as jnp
from jax import lax
from jax.experimental import pallas as pl
from jax.experimental.pallas import tpu as pltpu
from jax.sharding import Mesh, PartitionSpec as P

AXES = ("ylo", "core", "z", "x", "yhi")
FIRST = 10
WIN = 40
SWAP = ((0, 1), (1, 0))
VMEM = pl.BlockSpec(memory_space=pltpu.VMEM)
SMEM = pl.BlockSpec(memory_space=pltpu.SMEM)


def product_kernel(at_ref, w, n00, n01, n10, n11, theirs, *refs):
    outs, rows_ref = refs[:4], refs[4]
    h, a, b, x = at_ref[0], at_ref[1], at_ref[2], at_ref[3]
    for dh in range(2):
        for k in range(4):
            for q in range(2):
                start = (k * 2 + q) * WIN
                rows_ref[dh, start : start + WIN, :] = w[q * 2 + (h + dh) % 2, (x + k) % 4].astype(jnp.float32)
    left = [rows_ref[dh].astype(jnp.bfloat16) for dh in range(2)]
    for da in range(2):
        for t in range(2):
            total = None
            for dh in range(2):
                near = theirs[dh * 2 + da] if t else ((n00, n01), (n10, n11))[dh][da][...]
                term = lax.dot_general(left[dh], near, (((1,), (1,)), ((), ())), preferred_element_type=jnp.float32)
                total = term if total is None else total + term
            cols = pl.multiple_of(((a + da) % 2) * 768 + ((b + t) % 2) * 384, 128)
            for k in range(4):
                outs[k][:, pl.ds(cols, 384)] = total[k * 2 * WIN : (k + 1) * 2 * WIN]


def product(at, w, near, theirs):
    part = jax.ShapeDtypeStruct((2 * WIN, 1536), jnp.float32)
    return pl.pallas_call(
        product_kernel,
        out_shape=(part,) * 4,
        in_specs=[SMEM] + [VMEM] * 6,
        out_specs=(VMEM,) * 4,
        scratch_shapes=[pltpu.VMEM((2, 8 * WIN, 256), jnp.float32)],
        compiler_params=pltpu.CompilerParams(vmem_limit_bytes=32 * 2**20),
        cost_estimate=pl.CostEstimate(flops=2 * 320 * 1536 * 512, bytes_accessed=4 * 2**20, transcendentals=0),
    )(at, w, *near, theirs)


def dot(left, right):
    return jnp.dot(left, right, preferred_element_type=jnp.float32).astype(jnp.bfloat16)


def shift(k):
    return [(i, (i + k) % 4) for i in range(4)]


def on_device(lower_block, solve_factor, schur_window):
    at = jnp.stack([lax.axis_index(n) for n in ("yhi", "ylo", "core", "x")])
    win = dot(lower_block[:WIN], solve_factor)
    w = jnp.broadcast_to(win[None], (8, WIN, 256))
    groups = [[(FIRST + 2 * i) % 16 + q for i in range(8)] for q in range(2)]
    w = lax.all_to_all(w, "z", 0, 0, tiled=True, axis_index_groups=groups)
    win, lower_block = lax.optimization_barrier((win, lower_block))
    panel = dot(lower_block, solve_factor)
    near = [
        panel,
        lax.ppermute(panel, "ylo", SWAP),
        lax.ppermute(panel, "yhi", SWAP),
        lax.ppermute(panel, ("ylo", "yhi"), [(i, 3 - i) for i in range(4)]),
    ]
    theirs = lax.ppermute(jnp.stack(near), "core", SWAP)
    w = jnp.roll(w, FIRST // 2, 0).reshape(1, 4, 2, WIN, 256).transpose(0, 2, 1, 3, 4)
    w = jnp.broadcast_to(w, (2, 2, 4, WIN, 256)).reshape(4, 4, WIN, 256)
    fours = [[z * 4 + i for i in range(4)] for z in range(8)]
    w = lax.all_to_all(w, ("z", "yhi"), 0, 0, tiled=True, axis_index_groups=fours)
    keep, *send = product(at, w, near, theirs)
    got = [lax.ppermute(send[k - 1], "x", shift(k)) for k in (2, 1, 3)]
    return schur_window - ((keep + got[1]) + (got[2] + got[0]))


def solution(mesh):
    fine = Mesh(mesh.devices.reshape(2, 2, 16, 4, 2), AXES)
    row, depth = ("ylo", "core"), ("x", "yhi")
    out = P(row + depth, "z")
    return jax.shard_map(
        on_device, mesh=fine, in_specs=(P(("z",) + row, None), P(None, depth), out), out_specs=out, check_vma=False
    )
```

```python
import jax
import jax.numpy as jnp
from jax import lax
from jax.experimental import pallas as pl
from jax.experimental.pallas import tpu as pltpu
from jax.sharding import Mesh, PartitionSpec as P

AXES = ("ylo", "core", "z", "x", "yhi")
FIRST = 12
WIN = 40
SWAP = ((0, 1), (1, 0))
VMEM = pl.BlockSpec(memory_space=pltpu.VMEM)
SMEM = pl.BlockSpec(memory_space=pltpu.SMEM)


def product_kernel(at_ref, w, n00, n01, n10, n11, theirs, *refs):
    outs, rows_ref = refs[:4], refs[4]
    h, a, b, x = at_ref[0], at_ref[1], at_ref[2], at_ref[3]
    for dh in range(2):
        for k in range(4):
            for q in range(2):
                start = (k * 2 + q) * WIN
                rows_ref[dh, start : start + WIN, :] = w[q * 2 + (h + dh) % 2, (x + k) % 4].astype(jnp.float32)
    left = [rows_ref[dh].astype(jnp.bfloat16) for dh in range(2)]
    for da in range(2):
        for t in range(2):
            total = None
            for dh in range(2):
                near = theirs[dh * 2 + da] if t else ((n00, n01), (n10, n11))[dh][da][...]
                term = lax.dot_general(left[dh], near, (((1,), (1,)), ((), ())), preferred_element_type=jnp.float32)
                total = term if total is None else total + term
            cols = pl.multiple_of(((a + da) % 2) * 768 + ((b + t) % 2) * 384, 128)
            for k in range(4):
                outs[k][:, pl.ds(cols, 384)] = total[k * 2 * WIN : (k + 1) * 2 * WIN]


def product(at, w, near, theirs):
    part = jax.ShapeDtypeStruct((2 * WIN, 1536), jnp.float32)
    return pl.pallas_call(
        product_kernel,
        out_shape=(part,) * 4,
        in_specs=[SMEM] + [VMEM] * 6,
        out_specs=(VMEM,) * 4,
        scratch_shapes=[pltpu.VMEM((2, 8 * WIN, 256), jnp.float32)],
        compiler_params=pltpu.CompilerParams(vmem_limit_bytes=32 * 2**20),
        cost_estimate=pl.CostEstimate(flops=2 * 320 * 1536 * 512, bytes_accessed=4 * 2**20, transcendentals=0),
    )(at, w, *near, theirs)


def window_kernel(lower, factor, out_ref):
    rows = jnp.dot(lower[...], factor[...], preferred_element_type=jnp.float32)[:WIN].astype(jnp.bfloat16)
    for i in range(8):
        out_ref[i] = rows


def window(lower_block, solve_factor):
    inner, columns = solve_factor.shape
    return pl.pallas_call(
        window_kernel,
        out_shape=jax.ShapeDtypeStruct((8, WIN, columns), jnp.bfloat16),
        grid=(1,),
        in_specs=[pl.BlockSpec((48, inner), lambda i: (0, 0)), pl.BlockSpec((inner, columns), lambda i: (0, 0))],
        out_specs=pl.BlockSpec((8, WIN, columns), lambda i: (0, 0, 0)),
        compiler_params=pltpu.CompilerParams(vmem_limit_bytes=60 * 2**20),
        cost_estimate=pl.CostEstimate(flops=2 * 48 * inner * columns, bytes_accessed=2**20, transcendentals=0),
    )(lower_block, solve_factor)


def dot(left, right):
    return jnp.dot(left, right, preferred_element_type=jnp.float32).astype(jnp.bfloat16)


def shift(k):
    return [(i, (i + k) % 4) for i in range(4)]


def on_device(lower_block, solve_factor, schur_window):
    at = jnp.stack([lax.axis_index(n) for n in ("yhi", "ylo", "core", "x")])
    w = window(lower_block, solve_factor)
    w, lower_block = lax.optimization_barrier((w, lower_block))
    groups = [[(FIRST + 2 * i) % 16 + q for i in range(8)] for q in range(2)]
    w = lax.all_to_all(w, "z", 0, 0, tiled=True, axis_index_groups=groups)
    panel = dot(lower_block, solve_factor)
    near = [
        panel,
        lax.ppermute(panel, "ylo", SWAP),
        lax.ppermute(panel, "yhi", SWAP),
        lax.ppermute(panel, ("ylo", "yhi"), [(i, 3 - i) for i in range(4)]),
    ]
    theirs = lax.ppermute(jnp.stack(near), "core", SWAP)
    w = jnp.roll(w, FIRST // 2, 0).reshape(1, 4, 2, WIN, 256).transpose(0, 2, 1, 3, 4)
    w = jnp.broadcast_to(w, (2, 2, 4, WIN, 256)).reshape(4, 4, WIN, 256)
    fours = [[z * 4 + i for i in range(4)] for z in range(8)]
    w = lax.all_to_all(w, ("z", "yhi"), 0, 0, tiled=True, axis_index_groups=fours)
    keep, *send = product(at, w, near, theirs)
    got = [lax.ppermute(send[k - 1], "x", shift(k)) for k in (2, 1, 3)]
    return schur_window - ((keep + got[1]) + (got[2] + got[0]))


def solution(mesh):
    fine = Mesh(mesh.devices.reshape(2, 2, 16, 4, 2), AXES)
    row, depth = ("ylo", "core"), ("x", "yhi")
    out = P(row + depth, "z")
    return jax.shard_map(
        on_device, mesh=fine, in_specs=(P(("z",) + row, None), P(None, depth), out), out_specs=out, check_vma=False
    )
```

```python
import functools

import jax
import jax.numpy as jnp
from jax import lax
from jax.experimental import pallas as pl
from jax.experimental.pallas import tpu as pltpu
from jax.sharding import Mesh, PartitionSpec as P

AXES = ("ylo", "core", "z", "x", "yhi")
FIRST = 12
WIN = 40
SWAP = ((0, 1), (1, 0))
VMEM = pl.BlockSpec(memory_space=pltpu.VMEM)
SMEM = pl.BlockSpec(memory_space=pltpu.SMEM)


def product_kernel(first, at_ref, w, *refs):
    near = refs[:4] if first else [refs[0].at[i] for i in range(4)]
    outs, rows_ref = refs[-5:-1], refs[-1]
    h, a, b, x = at_ref[0], at_ref[1], at_ref[2], at_ref[3]
    for dh in range(2):
        for k in range(4):
            for q in range(2):
                start = (k * 2 + q) * WIN
                rows_ref[dh, start : start + WIN, :] = w[q * 2 + (h + dh) % 2, (x + k) % 4].astype(jnp.float32)
    left = [rows_ref[dh].astype(jnp.bfloat16) for dh in range(2)]
    for da in range(2):
        total = None
        for dh in range(2):
            term = lax.dot_general(left[dh], near[dh * 2 + da][...], (((1,), (1,)), ((), ())), preferred_element_type=jnp.float32)
            total = term if total is None else total + term
        cols = pl.multiple_of(((a + da) % 2) * 768 + ((b + (0 if first else 1)) % 2) * 384, 128)
        for k in range(4):
            outs[k][:, pl.ds(cols, 384)] = total[k * 2 * WIN : (k + 1) * 2 * WIN]


def product(at, w, near, into=()):
    part = jax.ShapeDtypeStruct((2 * WIN, 1536), jnp.float32)
    first = not into
    return pl.pallas_call(
        functools.partial(product_kernel, first),
        out_shape=(part,) * 4,
        in_specs=[SMEM] + [VMEM] * (1 + len(near) + len(into)),
        out_specs=(VMEM,) * 4,
        scratch_shapes=[pltpu.VMEM((2, 8 * WIN, 256), jnp.float32)],
        input_output_aliases={2 + len(near) + i: i for i in range(len(into))},
        compiler_params=pltpu.CompilerParams(vmem_limit_bytes=32 * 2**20),
        cost_estimate=pl.CostEstimate(flops=2 * 320 * 768 * 512, bytes_accessed=2 * 2**20, transcendentals=0),
    )(at, w, *near, *into)


def window_kernel(lower, factor, out_ref):
    rows = jnp.dot(lower[...], factor[...], preferred_element_type=jnp.float32)[:WIN].astype(jnp.bfloat16)
    for i in range(8):
        out_ref[i] = rows


def window(lower_block, solve_factor):
    inner, columns = solve_factor.shape
    return pl.pallas_call(
        window_kernel,
        out_shape=jax.ShapeDtypeStruct((8, WIN, columns), jnp.bfloat16),
        grid=(1,),
        in_specs=[pl.BlockSpec((48, inner), lambda i: (0, 0)), pl.BlockSpec((inner, columns), lambda i: (0, 0))],
        out_specs=pl.BlockSpec((8, WIN, columns), lambda i: (0, 0, 0)),
        compiler_params=pltpu.CompilerParams(vmem_limit_bytes=60 * 2**20),
        cost_estimate=pl.CostEstimate(flops=2 * 48 * inner * columns, bytes_accessed=2**20, transcendentals=0),
    )(lower_block, solve_factor)


def dot(left, right):
    return jnp.dot(left, right, preferred_element_type=jnp.float32).astype(jnp.bfloat16)


def shift(k):
    return [(i, (i + k) % 4) for i in range(4)]


def on_device(lower_block, solve_factor, schur_window):
    at = jnp.stack([lax.axis_index(n) for n in ("yhi", "ylo", "core", "x")])
    w = window(lower_block, solve_factor)
    w, lower_block = lax.optimization_barrier((w, lower_block))
    groups = [[(FIRST + 4 * i + 2 * h) % 16 + q for h in range(2) for i in range(4)] for q in range(2)]
    w = lax.all_to_all(w, "z", 0, 0, tiled=True, axis_index_groups=groups)
    panel = dot(lower_block, solve_factor)
    near = [
        panel,
        lax.ppermute(panel, "ylo", SWAP),
        lax.ppermute(panel, "yhi", SWAP),
        lax.ppermute(panel, ("ylo", "yhi"), [(i, 3 - i) for i in range(4)]),
    ]
    theirs = lax.ppermute(jnp.stack(near), "core", SWAP)
    w = jnp.roll(w.reshape(2, 4, WIN, 256), FIRST // 4, 1)
    w = jnp.broadcast_to(w[None], (2, 2, 4, WIN, 256)).reshape(4, 4, WIN, 256)
    fours = [[z * 4 + i for i in range(4)] for z in range(8)]
    w = lax.all_to_all(w, ("z", "yhi"), 0, 0, tiled=True, axis_index_groups=fours)
    keep, *send = product(at, w, [theirs], product(at, w, near))
    got = [lax.ppermute(send[k - 1], "x", shift(k)) for k in (2, 1, 3)]
    return schur_window - ((keep + got[1]) + (got[2] + got[0]))


def solution(mesh):
    fine = Mesh(mesh.devices.reshape(2, 2, 16, 4, 2), AXES)
    row, depth = ("ylo", "core"), ("x", "yhi")
    out = P(row + depth, "z")
    return jax.shard_map(
        on_device, mesh=fine, in_specs=(P(("z",) + row, None), P(None, depth), out), out_specs=out, check_vma=False
    )
```

```python
import functools

import jax
import jax.numpy as jnp
from jax import lax
from jax.experimental import pallas as pl
from jax.experimental.pallas import tpu as pltpu
from jax.sharding import Mesh, PartitionSpec as P

AXES = ("ylo", "core", "z", "x", "yhi")
FIRST = 12
WIN = 40
SWAP = ((0, 1), (1, 0))
VMEM = pl.BlockSpec(memory_space=pltpu.VMEM)
SMEM = pl.BlockSpec(memory_space=pltpu.SMEM)


def product_kernel(first, at_ref, w, *refs):
    near = refs[:4] if first else [refs[0].at[i] for i in range(4)]
    outs, rows_ref = refs[-5:-1], refs[-1]
    h, a, b, x = at_ref[0], at_ref[1], at_ref[2], at_ref[3]
    for dh in range(2):
        for k in range(4):
            for q in range(2):
                start = (k * 2 + q) * WIN
                rows_ref[dh, start : start + WIN, :] = w[q * 2 + (h + dh) % 2, (x + k) % 4].astype(jnp.float32)
    left = [rows_ref[dh].astype(jnp.bfloat16) for dh in range(2)]
    for da in range(2):
        total = None
        for dh in range(2):
            term = lax.dot_general(left[dh], near[dh * 2 + da][...], (((1,), (1,)), ((), ())), preferred_element_type=jnp.float32)
            total = term if total is None else total + term
        where = (a + da) % 2
        cols = where * 384 if first else where * 768 + (1 - b) * 384
        for k in range(4):
            outs[k][:, pl.ds(pl.multiple_of(cols, 128), 384)] = total[k * 2 * WIN : (k + 1) * 2 * WIN]
    if not first:
        for k in range(4):
            for y in range(2):
                cols = pl.ds(pl.multiple_of(y * 768 + b * 384, 128), 384)
                outs[k][:, cols] = refs[1 + k][:, y * 384 : (y + 1) * 384]


def product(at, w, near, into=()):
    first = not into
    part = jax.ShapeDtypeStruct((2 * WIN, 768 if first else 1536), jnp.float32)
    return pl.pallas_call(
        functools.partial(product_kernel, first),
        out_shape=(part,) * 4,
        in_specs=[SMEM] + [VMEM] * (1 + len(near) + len(into)),
        out_specs=(VMEM,) * 4,
        scratch_shapes=[pltpu.VMEM((2, 8 * WIN, 256), jnp.float32)],
        compiler_params=pltpu.CompilerParams(vmem_limit_bytes=32 * 2**20),
        cost_estimate=pl.CostEstimate(flops=2 * 320 * 768 * 512, bytes_accessed=2 * 2**20, transcendentals=0),
    )(at, w, *near, *into)


def window_kernel(lower, factor, out_ref):
    rows = jnp.dot(lower[...], factor[...], preferred_element_type=jnp.float32)[:WIN].astype(jnp.bfloat16)
    for i in range(8):
        out_ref[i] = rows


def window(lower_block, solve_factor):
    inner, columns = solve_factor.shape
    return pl.pallas_call(
        window_kernel,
        out_shape=jax.ShapeDtypeStruct((8, WIN, columns), jnp.bfloat16),
        grid=(1,),
        in_specs=[pl.BlockSpec((48, inner), lambda i: (0, 0)), pl.BlockSpec((inner, columns), lambda i: (0, 0))],
        out_specs=pl.BlockSpec((8, WIN, columns), lambda i: (0, 0, 0)),
        compiler_params=pltpu.CompilerParams(vmem_limit_bytes=60 * 2**20),
        cost_estimate=pl.CostEstimate(flops=2 * 48 * inner * columns, bytes_accessed=2**20, transcendentals=0),
    )(lower_block, solve_factor)


def dot(left, right):
    return jnp.dot(left, right, preferred_element_type=jnp.float32).astype(jnp.bfloat16)


def shift(k):
    return [(i, (i + k) % 4) for i in range(4)]


def on_device(lower_block, solve_factor, schur_window):
    at = jnp.stack([lax.axis_index(n) for n in ("yhi", "ylo", "core", "x")])
    w = window(lower_block, solve_factor)
    w, lower_block = lax.optimization_barrier((w, lower_block))
    groups = [[(FIRST + 4 * i + 2 * h) % 16 + q for h in range(2) for i in range(4)] for q in range(2)]
    w = lax.all_to_all(w, "z", 0, 0, tiled=True, axis_index_groups=groups)
    panel = dot(lower_block, solve_factor)
    near = [
        panel,
        lax.ppermute(panel, "ylo", SWAP),
        lax.ppermute(panel, "yhi", SWAP),
        lax.ppermute(panel, ("ylo", "yhi"), [(i, 3 - i) for i in range(4)]),
    ]
    theirs = lax.ppermute(jnp.stack(near), "core", SWAP)
    w = jnp.roll(w.reshape(2, 4, WIN, 256), FIRST // 4, 1)
    w = jnp.broadcast_to(w[None], (2, 2, 4, WIN, 256)).reshape(4, 4, WIN, 256)
    fours = [[z * 4 + i for i in range(4)] for z in range(8)]
    w = lax.all_to_all(w, ("z", "yhi"), 0, 0, tiled=True, axis_index_groups=fours)
    keep, *send = product(at, w, [theirs], product(at, w, near))
    got = [lax.ppermute(send[k - 1], "x", shift(k)) for k in (2, 1, 3)]
    return schur_window - ((keep + got[1]) + (got[2] + got[0]))


def solution(mesh):
    fine = Mesh(mesh.devices.reshape(2, 2, 16, 4, 2), AXES)
    row, depth = ("ylo", "core"), ("x", "yhi")
    out = P(row + depth, "z")
    return jax.shard_map(
        on_device, mesh=fine, in_specs=(P(("z",) + row, None), P(None, depth), out), out_specs=out, check_vma=False
    )
```

```python
import functools

import jax
import jax.numpy as jnp
from jax import lax
from jax.experimental import pallas as pl
from jax.experimental.pallas import tpu as pltpu
from jax.sharding import Mesh, PartitionSpec as P

AXES = ("ylo", "core", "z", "x", "yhi")
FIRST = 12
WIN = 40
SWAP = ((0, 1), (1, 0))
VMEM = pl.BlockSpec(memory_space=pltpu.VMEM)
SMEM = pl.BlockSpec(memory_space=pltpu.SMEM)


def product_kernel(first, at_ref, w, *refs):
    near = refs[:4] if first else [refs[0].at[i] for i in range(4)]
    outs, rows_ref = refs[-5:-1], refs[-1]
    h, a, b, x = at_ref[0], at_ref[1], at_ref[2], at_ref[3]
    for dh in range(2):
        for k in range(4):
            for q in range(2):
                start = (k * 2 + q) * WIN
                rows_ref[dh, start : start + WIN, :] = w[q * 2 + (h + dh) % 2, (x + k) % 4].astype(jnp.float32)
    left = [rows_ref[dh].astype(jnp.bfloat16) for dh in range(2)]
    for da in range(2):
        total = None
        for dh in range(2):
            term = lax.dot_general(left[dh], near[dh * 2 + da][...], (((1,), (1,)), ((), ())), preferred_element_type=jnp.float32)
            total = term if total is None else total + term
        where = (a + da) % 2
        cols = where * 384 if first else where * 768 + (1 - b) * 384
        for k in range(4):
            outs[k][:, pl.ds(pl.multiple_of(cols, 128), 384)] = total[k * 2 * WIN : (k + 1) * 2 * WIN]
    if not first:
        for k in range(4):
            for y in range(2):
                cols = pl.ds(pl.multiple_of(y * 768 + b * 384, 128), 384)
                outs[k][:, cols] = refs[1 + k][:, y * 384 : (y + 1) * 384]


def product(at, w, near, into=()):
    first = not into
    part = jax.ShapeDtypeStruct((2 * WIN, 768 if first else 1536), jnp.float32)
    return pl.pallas_call(
        functools.partial(product_kernel, first),
        out_shape=(part,) * 4,
        in_specs=[SMEM] + [VMEM] * (1 + len(near) + len(into)),
        out_specs=(VMEM,) * 4,
        scratch_shapes=[pltpu.VMEM((2, 8 * WIN, 256), jnp.float32)],
        compiler_params=pltpu.CompilerParams(vmem_limit_bytes=32 * 2**20),
        cost_estimate=pl.CostEstimate(flops=2 * 320 * 768 * 512, bytes_accessed=2 * 2**20, transcendentals=0),
    )(at, w, *near, *into)


def window_kernel(lower, factor, out_ref):
    rows = jnp.dot(lower[...], factor[...], preferred_element_type=jnp.float32)[:WIN].astype(jnp.bfloat16)
    for i in range(8):
        out_ref[i] = rows


def window(lower_block, solve_factor):
    inner, columns = solve_factor.shape
    return pl.pallas_call(
        window_kernel,
        out_shape=jax.ShapeDtypeStruct((8, WIN, columns), jnp.bfloat16),
        grid=(1,),
        in_specs=[pl.BlockSpec((48, inner), lambda i: (0, 0)), pl.BlockSpec((inner, columns), lambda i: (0, 0))],
        out_specs=pl.BlockSpec((8, WIN, columns), lambda i: (0, 0, 0)),
        compiler_params=pltpu.CompilerParams(vmem_limit_bytes=60 * 2**20),
        cost_estimate=pl.CostEstimate(flops=2 * 48 * inner * columns, bytes_accessed=2**20, transcendentals=0),
    )(lower_block, solve_factor)


def dot(left, right):
    return jnp.dot(left, right, preferred_element_type=jnp.float32).astype(jnp.bfloat16)


def shift(k):
    return [(i, (i + k) % 4) for i in range(4)]


def on_device(lower_block, solve_factor, schur_window):
    at = jnp.stack([lax.axis_index(n) for n in ("yhi", "ylo", "core", "x")])
    w = window(lower_block, solve_factor)
    w, lower_block = lax.optimization_barrier((w, lower_block))
    groups = [[(FIRST + 4 * i + 2 * h) % 16 + q for h in range(2) for i in range(4)] for q in range(2)]
    w = lax.all_to_all(w, "z", 0, 0, tiled=True, axis_index_groups=groups)
    panel = dot(lower_block, solve_factor)
    near = [
        panel,
        lax.ppermute(panel, "ylo", SWAP),
        lax.ppermute(panel, "yhi", SWAP),
        lax.ppermute(panel, ("ylo", "yhi"), [(i, 3 - i) for i in range(4)]),
    ]
    theirs = lax.ppermute(jnp.stack(near), "core", SWAP)
    w = jnp.roll(w.reshape(2, 4, WIN, 256), FIRST // 4, 1)
    w = jnp.broadcast_to(w[None], (2, 2, 4, WIN, 256)).reshape(4, 4, WIN, 256)
    fours = [[z * 4 + i for i in range(4)] for z in range(8)]
    w = lax.all_to_all(w, ("z", "yhi"), 0, 0, tiled=True, axis_index_groups=fours)
    keep, *send = product(at, w, [theirs], product(at, w, near))
    got = [lax.ppermute(send[k - 1], "x", shift(k)) for k in (2, 1, 3)]
    part = lax.optimization_barrier(schur_window - (keep + got[0]))
    return part - (got[1] + got[2])


def solution(mesh):
    fine = Mesh(mesh.devices.reshape(2, 2, 16, 4, 2), AXES)
    row, depth = ("ylo", "core"), ("x", "yhi")
    out = P(row + depth, "z")
    return jax.shard_map(
        on_device, mesh=fine, in_specs=(P(("z",) + row, None), P(None, depth), out), out_specs=out, check_vma=False
    )
```

```python
import functools

import jax
import jax.numpy as jnp
from jax import lax
from jax.experimental import pallas as pl
from jax.experimental.pallas import tpu as pltpu
from jax.sharding import Mesh, PartitionSpec as P

AXES = ("ylo", "core", "z", "x", "yhi")
FIRST = 12
WIN = 40
SWAP = ((0, 1), (1, 0))
VMEM = pl.BlockSpec(memory_space=pltpu.VMEM)
SMEM = pl.BlockSpec(memory_space=pltpu.SMEM)


def product_kernel(first, at_ref, w, *refs):
    near = refs[:4] if first else [refs[0].at[i] for i in range(4)]
    outs, rows_ref = refs[-5:-1], refs[-1]
    h, a, b, x = at_ref[0], at_ref[1], at_ref[2], at_ref[3]
    for dh in range(2):
        for k in range(4):
            for q in range(2):
                start = (k * 2 + q) * WIN
                rows_ref[dh, start : start + WIN, :] = w[q * 2 + (h + dh) % 2, (x + k) % 4].astype(jnp.float32)
    left = [rows_ref[dh].astype(jnp.bfloat16) for dh in range(2)]
    for da in range(2):
        total = None
        for dh in range(2):
            term = lax.dot_general(left[dh], near[dh * 2 + da][...], (((1,), (1,)), ((), ())), preferred_element_type=jnp.float32)
            total = term if total is None else total + term
        where = (a + da) % 2
        cols = where * 384 if first else where * 768 + (1 - b) * 384
        for k in range(4):
            outs[k][:, pl.ds(pl.multiple_of(cols, 128), 384)] = total[k * 2 * WIN : (k + 1) * 2 * WIN]
    if not first:
        for k in range(4):
            for y in range(2):
                cols = pl.ds(pl.multiple_of(y * 768 + b * 384, 128), 384)
                outs[k][:, cols] = refs[1 + k][:, y * 384 : (y + 1) * 384]


def product(at, w, near, into=()):
    first = not into
    part = jax.ShapeDtypeStruct((2 * WIN, 768 if first else 1536), jnp.float32)
    return pl.pallas_call(
        functools.partial(product_kernel, first),
        out_shape=(part,) * 4,
        in_specs=[SMEM] + [VMEM] * (1 + len(near) + len(into)),
        out_specs=(VMEM,) * 4,
        scratch_shapes=[pltpu.VMEM((2, 8 * WIN, 256), jnp.float32)],
        compiler_params=pltpu.CompilerParams(vmem_limit_bytes=32 * 2**20),
        cost_estimate=pl.CostEstimate(flops=2 * 320 * 768 * 512, bytes_accessed=2 * 2**20, transcendentals=0),
    )(at, w, *near, *into)


def window_kernel(lower, factor, out_ref):
    rows = jnp.dot(lower[...], factor[...], preferred_element_type=jnp.float32)[:WIN].astype(jnp.bfloat16)
    for i in range(8):
        out_ref[i] = rows


def window(lower_block, solve_factor):
    inner, columns = solve_factor.shape
    return pl.pallas_call(
        window_kernel,
        out_shape=jax.ShapeDtypeStruct((8, WIN, columns), jnp.bfloat16),
        grid=(1,),
        in_specs=[pl.BlockSpec((48, inner), lambda i: (0, 0)), pl.BlockSpec((inner, columns), lambda i: (0, 0))],
        out_specs=pl.BlockSpec((8, WIN, columns), lambda i: (0, 0, 0)),
        compiler_params=pltpu.CompilerParams(vmem_limit_bytes=60 * 2**20),
        cost_estimate=pl.CostEstimate(flops=2 * 48 * inner * columns, bytes_accessed=2**20, transcendentals=0),
    )(lower_block, solve_factor)


def dot(left, right):
    return jnp.dot(left, right, preferred_element_type=jnp.float32).astype(jnp.bfloat16)


def shift(k):
    return [(i, (i + k) % 4) for i in range(4)]


def on_device(lower_block, solve_factor, schur_window):
    at = jnp.stack([lax.axis_index(n) for n in ("yhi", "ylo", "core", "x")])
    w = window(lower_block, solve_factor)
    w, lower_block = lax.optimization_barrier((w, lower_block))
    groups = [[(FIRST + 4 * i + 2 * h) % 16 + q for h in range(2) for i in range(4)] for q in range(2)]
    w = lax.all_to_all(w, "z", 0, 0, tiled=True, axis_index_groups=groups)
    panel = dot(lower_block, solve_factor)
    near = [
        panel,
        lax.ppermute(panel, "ylo", SWAP),
        lax.ppermute(panel, "yhi", SWAP),
        lax.ppermute(panel, ("ylo", "yhi"), [(i, 3 - i) for i in range(4)]),
    ]
    near[1], near[2] = lax.optimization_barrier((near[1], near[2]))
    theirs = lax.ppermute(jnp.stack(near), "core", SWAP)
    w = jnp.roll(w.reshape(2, 4, WIN, 256), FIRST // 4, 1)
    w = jnp.broadcast_to(w[None], (2, 2, 4, WIN, 256)).reshape(4, 4, WIN, 256)
    fours = [[z * 4 + i for i in range(4)] for z in range(8)]
    w = lax.all_to_all(w, ("z", "yhi"), 0, 0, tiled=True, axis_index_groups=fours)
    keep, *send = product(at, w, [theirs], product(at, w, near))
    got = [lax.ppermute(send[k - 1], "x", shift(k)) for k in (2, 1, 3)]
    part = lax.optimization_barrier(schur_window - (keep + got[0]))
    return part - (got[1] + got[2])


def solution(mesh):
    fine = Mesh(mesh.devices.reshape(2, 2, 16, 4, 2), AXES)
    row, depth = ("ylo", "core"), ("x", "yhi")
    out = P(row + depth, "z")
    return jax.shard_map(
        on_device, mesh=fine, in_specs=(P(("z",) + row, None), P(None, depth), out), out_specs=out, check_vma=False
    )
```
